32 devices in a mesh: lat: 8 (over z, y), lon: 2 (over x), comp: 2 (over core).
Axes of the slice: x: 2, y: 2, z: 4, core: 2. Of those that a mesh axis runs over, the one named last changes fastest.
Arguments:
- atm_state: bfloat16 [2, 16, 512, 384], P(None, 'lat', ('lon', 'comp')), may hold values from -6 to 6
- ocean_prev: bfloat16 [2, 16, 512, 128], P(None, 'lat', ('lon', 'comp')), may hold values from -6 to 6
- land_sea: int32 [16, 512], P('lat', ('lon', 'comp')), may hold values 0 or 1
- window_ids: int32 [16, 512], P('lat', ('lon', 'comp')), may hold values from 0 to 511, as said below
- conv_atm: float32 [2, 3, 3, 384], replicated, may hold values from -2 to 2
- attn_gain: float32 [2, 384], replicated, may hold values from 0.5 to 2
- qkv_matrix: bfloat16 [2, 384, 1152], replicated, may hold values from -0.3125 to 0.3125
- attn_scales: float32 [2, 6], replicated, may hold values from 4 to 32
- out_matrix: bfloat16 [2, 384, 384], replicated, may hold values from -0.3125 to 0.3125
- mlp_gain: float32 [2, 384], replicated, may hold values from 0.5 to 2
- member_in: float32 [2, 2, 384], replicated, may hold values from 0.5 to 2
- member_out: float32 [2, 2, 1536], replicated, may hold values from 0.5 to 2
- up_matrix: bfloat16 [2, 384, 1536], replicated, may hold values from -0.3125 to 0.3125
- down_matrix: bfloat16 [2, 1536, 384], replicated, may hold values from -0.15625 to 0.15625
- flux_matrix: bfloat16 [384, 128], replicated, may hold values from -0.3125 to 0.3125
- conv_ocean: float32 [3, 3, 3, 128], replicated, may hold values from -2 to 2
- point_matrix: bfloat16 [3, 128, 128], replicated, may hold values from -0.5 to 0.5
- ocean_gain: float32 [128], replicated, may hold values from 0.5 to 2
- ocean_qkv: bfloat16 [128, 384], replicated, may hold values from -0.5 to 0.5
- ocean_scale: float32 [2], replicated, may hold values from 4 to 32
- ocean_out: bfloat16 [128, 128], replicated, may hold values from -0.5 to 0.5
- seaside_return_matrix: bfloat16 [128, 384], replicated, may hold values from -0.5 to 0.5
Outputs:
- updated_airflow_field: bfloat16 [2, 16, 512, 384], P(None, 'lat', ('lon', 'comp'))
- updated_seaside_channels: bfloat16 [2, 16, 512, 128], P(None, 'lat', ('lon', 'comp'))
The draws below stay inside these ranges and needn't reach their ends.
Inputs may be any that keep to these rules, and one draw needn't show every extreme that they name: `land_sea`: 1 marks a sea column, 0 land. `window_ids`: along each latitude the value is the longitude of the first column of that column's window; it never falls along a row, every window lies inside an aligned run of 128 longitudes, and the last longitude of every row is a window of its own.
All inputs are finite; a program needn't handle non-finite values. No bound on the sum of `land_sea` on one device may be relied on, other than what follows from the above.
Results may differ from the reference program's by a relative error of at most 0.018.
Values may be sent and summed in bfloat16 or wider, within the bound.
A program may use at most 64 MiB of HBM per device.

```python
import math
import jax
import jax.numpy as jnp
from jax import lax

WIDTH = 384
HEADS = 6
HIDDEN_SIZE = 1536
OCEAN = 128
OHEADS = 2
BLOCKS = 2
MEMBERS = 2
COLS_DEV = 128
NLAT = 16
NLON = 512


def draw_window_ids(key, part):
    break_draw = jax.random.randint(key, (NLAT, NLON), 0, 12)
    lon_index = jnp.arange(NLON, dtype=jnp.int32)
    block_start = lon_index % COLS_DEV == 0
    last_column = lon_index == NLON - 1
    starts = (break_draw == 0) | block_start[None, :] | last_column[None, :]
    marked = jnp.where(starts, lon_index[None, :], 0)
    return lax.cummax(marked, axis=1).astype(jnp.int32)


def place_ends(values, rng, smallest, largest):
    spot = [jax.random.randint(jax.random.fold_in(rng, axis), (), 0, length) for axis, length in enumerate(values.shape)]
    widest = values.shape.index(max(values.shape))
    beside = spot[:widest] + [(spot[widest] + 1) % values.shape[widest]] + spot[widest + 1:]
    return values.at[tuple(spot)].set(smallest).at[tuple(beside)].set(largest)


def levels(key, extent, pieces, smallest, high):
    def one(axis_at, parts):
        draws = jax.random.uniform(jax.random.fold_in(jax.random.fold_in(key, 6), axis_at), (parts,), jnp.float32, smallest / len(pieces), high / len(pieces))
        return jnp.repeat(jnp.exp(draws), extent[axis_at] // parts).reshape((-1,) + (1,) * (len(extent) - axis_at - 1))

    factor_of = one(*pieces[0])
    for cut in pieces[1:]:
        factor_of = factor_of * one(*cut)
    return factor_of


def bell_draw(rng, dims, scale, reach, split=(), kind=jnp.bfloat16):
    array = jax.random.normal(rng, dims, jnp.float32) * scale
    if len(split) > 0:
        array = levels(rng, dims, split, -0.22, 0.18) * array
    return jnp.clip(array, min=-reach, max=reach).astype(kind)


def setup_inputs(seed: int = 0) -> dict:
    keys = jax.random.split(jax.random.key(seed), 23)
    return {
        "atm_state": bell_draw(keys[0], (MEMBERS, NLAT, NLON, WIDTH), 1.0, 6.0, ((1, 8), (2, 4))),
        "ocean_prev": bell_draw(keys[1], (MEMBERS, NLAT, NLON, OCEAN), 1.0, 6.0, ((1, 8), (2, 4))),
        "land_sea": place_ends((jax.random.randint(keys[2], (NLAT, NLON), 0, 10) < 7).astype(jnp.int32), jax.random.fold_in(keys[2], 1), 0, 1),
        "window_ids": draw_window_ids(jax.random.fold_in(keys[22], 71), 0),
        "conv_atm": bell_draw(keys[4], (BLOCKS, 3, 3, WIDTH), 0.35, 2.0, (), jnp.float32),
        "attn_gain": jnp.clip(jnp.exp(jax.random.uniform(keys[5], (BLOCKS, WIDTH), jnp.float32, math.log(0.5), math.log(2.0))), 0.5, 2.0),
        "qkv_matrix": bell_draw(keys[6], (BLOCKS, WIDTH, 3 * WIDTH), WIDTH ** -0.5, 0.3125),
        "attn_scales": jnp.clip(jnp.exp(jax.random.uniform(keys[7], (BLOCKS, HEADS), jnp.float32, math.log(4.0), math.log(32.0))), 4.0, 32.0),
        "out_matrix": bell_draw(keys[8], (BLOCKS, WIDTH, WIDTH), WIDTH ** -0.5, 0.3125),
        "mlp_gain": jnp.clip(jnp.exp(jax.random.uniform(keys[9], (BLOCKS, WIDTH), jnp.float32, math.log(0.5), math.log(2.0))), 0.5, 2.0),
        "member_in": jnp.clip(jnp.exp(jax.random.uniform(keys[10], (BLOCKS, MEMBERS, WIDTH), jnp.float32, math.log(0.5), math.log(2.0))), 0.5, 2.0),
        "member_out": jnp.clip(jnp.exp(jax.random.uniform(keys[11], (BLOCKS, MEMBERS, HIDDEN_SIZE), jnp.float32, math.log(0.5), math.log(2.0))), 0.5, 2.0),
        "up_matrix": bell_draw(keys[12], (BLOCKS, WIDTH, HIDDEN_SIZE), WIDTH ** -0.5, 0.3125),
        "down_matrix": bell_draw(keys[13], (BLOCKS, HIDDEN_SIZE, WIDTH), HIDDEN_SIZE ** -0.5, 0.15625),
        "flux_matrix": bell_draw(keys[14], (WIDTH, OCEAN), WIDTH ** -0.5, 0.3125),
        "conv_ocean": bell_draw(keys[15], (3, 3, 3, OCEAN), 0.35, 2.0, (), jnp.float32),
        "point_matrix": bell_draw(keys[16], (3, OCEAN, OCEAN), OCEAN ** -0.5, 0.5),
        "ocean_gain": jnp.clip(jnp.exp(jax.random.uniform(keys[17], (OCEAN,), jnp.float32, math.log(0.5), math.log(2.0))), 0.5, 2.0),
        "ocean_qkv": bell_draw(keys[18], (OCEAN, 3 * OCEAN), OCEAN ** -0.5, 0.5),
        "ocean_scale": jnp.clip(jnp.exp(jax.random.uniform(keys[19], (OHEADS,), jnp.float32, math.log(4.0), math.log(32.0))), 4.0, 32.0),
        "ocean_out": bell_draw(keys[20], (OCEAN, OCEAN), OCEAN ** -0.5, 0.5),
        "seaside_return_matrix": bell_draw(keys[21], (OCEAN, WIDTH), OCEAN ** -0.5, 0.5),
    }


NORM_EPS = 1e-05
UNIT_EPS = 1e-06

def damped_model_field(values_in):
    return lax.optimization_barrier(values_in.astype(jnp.bfloat16))

def smooth(values_in):
    return jax.nn.gelu(values_in, approximate=False)

def layer_norm(values_in, gain_vector):
    widened = values_in.astype(jnp.float32)
    centred = widened - lax.optimization_barrier(jnp.mean(widened, axis=-1, keepdims=True))
    spread = lax.optimization_barrier(jnp.mean(centred * centred, axis=-1, keepdims=True))
    return centred * lax.rsqrt(spread + NORM_EPS) * gain_vector

def unit_heads(projected, head_count):
    shaped = projected.reshape(projected.shape[:-1] + (head_count, projected.shape[-1] // head_count))
    shaped = shaped * lax.rsqrt(lax.optimization_barrier(jnp.mean(shaped * shaped, axis=-1, keepdims=True)) + UNIT_EPS)
    return damped_model_field(shaped.reshape(projected.shape))

def nine_taps(padded, kernel):
    row_count = padded.shape[1] - 2
    col_count = padded.shape[2] - 2
    accum = jnp.zeros((padded.shape[0], row_count, col_count, padded.shape[3]), jnp.float32)
    for lat_shift in range(3):
        for lon_shift in range(3):
            window = padded[:, lat_shift:lat_shift + row_count, lon_shift:lon_shift + col_count]
            accum = accum + window.astype(jnp.float32) * kernel[lat_shift, lon_shift]
    return accum

def global_conv(values_in, kernel):
    padded = jnp.pad(values_in, ((0, 0), (1, 1), (0, 0), (0, 0)))
    padded = jnp.concatenate([padded[:, :, -1:], padded, padded[:, :, :1]], axis=2)
    return nine_taps(padded, kernel)

def window_attend(query_units, key_units, value_rows, window_ids, head_scale):
    members, row_count, length, channels = query_units.shape
    head_count = head_scale.shape[0]
    head_dim = channels // head_count
    blocks = length // COLS_DEV
    shape_six = (members, row_count, blocks, COLS_DEV, head_count, head_dim)
    query_six = query_units.reshape(shape_six).astype(jnp.float32)
    key_six = key_units.reshape(shape_six).astype(jnp.float32)
    value_six = value_rows.reshape(shape_six).astype(jnp.float32)
    id_blocks = window_ids.reshape(row_count, blocks, COLS_DEV)
    same_window = id_blocks[:, :, :, None] == id_blocks[:, :, None, :]
    scores = jnp.einsum('mrbqhd,mrbkhd->mrbhqk', query_six, key_six) * (head_scale / head_dim)[:, None, None]
    exp_terms = jnp.where(same_window[None, :, :, None], jnp.exp(scores), 0.0)
    denominator = lax.optimization_barrier(jnp.sum(exp_terms, axis=-1))
    numerator = jnp.einsum('mrbhqk,mrbkhd->mrbqhd', damped_model_field(exp_terms).astype(jnp.float32), value_six)
    result = numerator / jnp.transpose(denominator, (0, 1, 2, 4, 3))[..., None]
    return damped_model_field(result.reshape(members, row_count, length, channels))

def token_section(mixed_state, window_ids, attn_gain, qkv_matrix, attn_scales, out_matrix, mlp_gain, scale_in, scale_out, up_matrix, down_matrix):
    normed = damped_model_field(layer_norm(mixed_state, attn_gain))
    projected = jnp.dot(normed, qkv_matrix, preferred_element_type=jnp.float32)
    query_units = unit_heads(projected[..., :WIDTH], HEADS)
    key_units = unit_heads(projected[..., WIDTH:2 * WIDTH], HEADS)
    value_rows = damped_model_field(projected[..., 2 * WIDTH:])
    attended = window_attend(query_units, key_units, value_rows, window_ids, attn_scales)
    after_attn = damped_model_field(mixed_state.astype(jnp.float32) + jnp.dot(attended, out_matrix, preferred_element_type=jnp.float32))
    scaled = damped_model_field(layer_norm(after_attn, mlp_gain) * scale_in[:, None, None, :])
    lifted_channel_values = jnp.dot(scaled, up_matrix, preferred_element_type=jnp.float32) * scale_out[:, None, None, :]
    activated = damped_model_field(smooth(lifted_channel_values))
    return damped_model_field(after_attn.astype(jnp.float32) + jnp.dot(activated, down_matrix, preferred_element_type=jnp.float32))

def pool_pairs(values_in):
    members, row_count, col_count, channels = values_in.shape
    shaped = values_in.astype(jnp.float32).reshape(members, row_count // 2, 2, col_count // 2, 2, channels)
    return lax.optimization_barrier(jnp.mean(shaped, axis=(2, 4)))

def upsample(coarse):
    members, row_count, col_count, channels = coarse.shape
    spread_out = jnp.broadcast_to(coarse[:, :, None, :, None, :], (members, row_count, 2, col_count, 2, channels))
    return spread_out.reshape(members, 2 * row_count, 2 * col_count, channels)

def lat_terms(query_units, key_units, value_rows, head_scale):
    head_count = head_scale.shape[0]
    head_dim = query_units.shape[-1] // head_count
    query_five = query_units.reshape(query_units.shape[:-1] + (head_count, head_dim)).astype(jnp.float32)
    key_five = key_units.reshape(key_units.shape[:-1] + (head_count, head_dim)).astype(jnp.float32)
    value_five = value_rows.reshape(key_units.shape[:-1] + (head_count, head_dim)).astype(jnp.float32)
    scores = jnp.einsum('mijhd,mkjhd->mhikj', query_five, key_five) * (head_scale / head_dim)[None, :, None, None, None]
    exp_terms = jnp.exp(scores)
    denominator = lax.optimization_barrier(jnp.sum(exp_terms, axis=3))
    numerator = jnp.einsum('mhikj,mkjhd->mijhd', damped_model_field(exp_terms).astype(jnp.float32), value_five)
    return (numerator, denominator)

def finish_heads(numerator, denominator):
    result = numerator / jnp.transpose(denominator, (0, 2, 3, 1))[..., None]
    return damped_model_field(result.reshape(result.shape[:3] + (result.shape[3] * result.shape[4],)))

def ocean_trunk(marine_starting_field, conv_ocean, point_matrix, ocean_gain, ocean_qkv, ocean_scale, ocean_out):
    act_first = damped_model_field(global_conv(marine_starting_field, conv_ocean[0]))
    fine_first = damped_model_field(smooth(jnp.dot(act_first, point_matrix[0], preferred_element_type=jnp.float32)))
    coarse_start = damped_model_field(pool_pairs(fine_first))
    act_second = damped_model_field(global_conv(coarse_start, conv_ocean[1]))
    coarse_first = damped_model_field(smooth(jnp.dot(act_second, point_matrix[1], preferred_element_type=jnp.float32)))
    normed = damped_model_field(layer_norm(coarse_first, ocean_gain))
    projected = jnp.dot(normed, ocean_qkv, preferred_element_type=jnp.float32)
    query_units = unit_heads(projected[..., :OCEAN], OHEADS)
    key_units = unit_heads(projected[..., OCEAN:2 * OCEAN], OHEADS)
    value_rows = damped_model_field(projected[..., 2 * OCEAN:])
    numerator, denominator = lat_terms(query_units, key_units, value_rows, ocean_scale)
    attended = finish_heads(numerator, denominator)
    coarse_next = damped_model_field(coarse_first.astype(jnp.float32) + jnp.dot(attended, ocean_out, preferred_element_type=jnp.float32))
    merged = damped_model_field(fine_first.astype(jnp.float32) + upsample(coarse_next).astype(jnp.float32))
    return damped_model_field(global_conv(merged, conv_ocean[2]))

def reference(atm_state, ocean_prev, land_sea, window_ids, conv_atm, attn_gain, qkv_matrix, attn_scales, out_matrix, mlp_gain, member_in, member_out, up_matrix, down_matrix, flux_matrix, conv_ocean, point_matrix, ocean_gain, ocean_qkv, ocean_scale, ocean_out, seaside_return_matrix):
    current_model_field = atm_state
    for block_index in range(BLOCKS):
        mixed_state = damped_model_field(current_model_field.astype(jnp.float32) + global_conv(current_model_field, conv_atm[block_index]))

        def per_row(row_args):
            row_state, row_ids = row_args
            return token_section(row_state, row_ids, attn_gain[block_index], qkv_matrix[block_index], attn_scales[block_index], out_matrix[block_index], mlp_gain[block_index], member_in[block_index], member_out[block_index], up_matrix[block_index], down_matrix[block_index])
        rows_out = lax.map(per_row, (jnp.moveaxis(mixed_state, 1, 0)[:, :, None], window_ids[:, None, :]))
        current_model_field = jnp.moveaxis(rows_out[:, :, 0], 0, 1)
    marine_grid_indicator = land_sea.astype(jnp.float32)[None, :, :, None]
    flux_terms = jnp.dot(current_model_field, flux_matrix, preferred_element_type=jnp.float32)
    marine_starting_field = damped_model_field(marine_grid_indicator * (ocean_prev.astype(jnp.float32) + flux_terms))
    act_last = ocean_trunk(marine_starting_field, conv_ocean, point_matrix, ocean_gain, ocean_qkv, ocean_scale, ocean_out)
    lifted_channel_values = smooth(jnp.dot(act_last, point_matrix[2], preferred_element_type=jnp.float32))
    updated_seaside_channels = damped_model_field(marine_grid_indicator * (marine_starting_field.astype(jnp.float32) + lifted_channel_values))
    updated_airflow_field = damped_model_field(current_model_field.astype(jnp.float32) + marine_grid_indicator * jnp.dot(updated_seaside_channels, seaside_return_matrix, preferred_element_type=jnp.float32))
    return (updated_airflow_field, updated_seaside_channels)
```

```python
import functools

import jax
import jax.numpy as jnp
from jax import lax
from jax.experimental import pallas as pl
from jax.experimental.pallas import tpu as pltpu
from jax.sharding import PartitionSpec as P

NORM_EPS = 1e-05
UNIT_EPS = 1e-06
HEAD = 64
LANES = 128
RIM = 8
EDGE = 16
LOG2E = 1.4426950408889634
MESH = pl.DeviceIdType.MESH
F32 = jnp.float32
BF16 = jnp.bfloat16
SIDES = [(dy, dx) for dy in (-1, 0, 1) for dx in (-1, 0, 1) if (dy, dx) != (0, 0)]


def gelu(x):
    return 0.5 * x * (1.0 + lax.erf(x * 0.7071067811865476))


def layer_norm(x, gain):
    centred = x - jnp.mean(x, axis=-1, keepdims=True)
    spread = jnp.mean(centred * centred, axis=-1, keepdims=True)
    return centred * lax.rsqrt(spread + NORM_EPS) * gain


def dot(a, b):
    return jnp.dot(a, b, preferred_element_type=F32)


def unit(p, head_mean):
    mean_square = dot((p * p).astype(BF16), head_mean)
    return (p * lax.rsqrt(mean_square + UNIT_EPS)).astype(BF16)


def attend_pair(q, k, v, mask, scale_a, scale_b):
    n = q.shape[0]
    lane = lax.broadcasted_iota(jnp.int32, (1, LANES), 1)
    low = (lane < HEAD).astype(F32).astype(BF16)
    high = (lane >= HEAD).astype(F32).astype(BF16)
    keys = jnp.concatenate([k * low, k * high], axis=0)
    scores = lax.dot_general(q, keys, (((1,), (1,)), ((), ())), preferred_element_type=F32)
    both = lax.broadcasted_iota(jnp.int32, (1, 2 * n), 1)
    factor = jnp.where(both < n, scale_a, scale_b) * (LOG2E / HEAD)
    terms = jnp.exp2(scores * factor) * jnp.concatenate([mask, mask], axis=1)
    values = jnp.concatenate([v * low, v * high], axis=0)
    ones = jnp.concatenate(
        [jnp.broadcast_to(low, (n, LANES)), jnp.broadcast_to(high, (n, LANES))], axis=0
    )
    result = dot(terms.astype(BF16), jnp.concatenate([values, ones], axis=1))
    return (result[:, :LANES] / result[:, LANES:]).astype(BF16)


def kernel(
    sizes,
    atm_ref,
    prev_ref,
    sea_ref,
    ids_ref,
    conv_ref,
    attn_gain_ref,
    qkv_hbm,
    scales_ref,
    out_hbm,
    mlp_gain_ref,
    min_ref,
    mout_ref,
    up_hbm,
    down_hbm,
    flux_ref,
    oconv_ref,
    point_ref,
    ogain_ref,
    oqkv_ref,
    oscale_ref,
    oout_ref,
    return_ref,
    air_ref,
    seaside_ref,
    qkv,
    outw,
    up,
    down,
    cur,
    hrow,
    hcol,
    hcor,
    pad,
    mixed,
    attended,
    same,
    seab,
    start,
    startpad,
    senda,
    recva,
    edges,
    edger,
    opad,
    cpad,
    fine,
    sendb,
    recvb,
    act,
    wsem,
    hsend,
    hrecv,
    asend,
    arecv,
    esend,
    erecv,
    bsend,
    brecv,
):
    n_lat, n_lon, n_comp = sizes
    members, rows, length, width = atm_ref.shape
    blocks = conv_ref.shape[0]
    hidden = up.shape[2]
    piece = length // n_lat
    win = senda.shape[3]
    lats = n_lat * rows
    cells = rows * length
    chunks = width // LANES
    sectors = n_lon * n_comp
    lat = lax.axis_index("lat")
    sector = lax.axis_index("lon") * n_comp + lax.axis_index("comp")

    def place(lat_at, shift):
        at = (sector + shift + sectors) % sectors
        return {"lat": lat_at, "lon": at // n_comp, "comp": at % n_comp}

    copies = [
        pltpu.make_async_copy(source, target, wsem.at[i])
        for i, (source, target) in enumerate(
            ((qkv_hbm, qkv), (out_hbm, outw), (up_hbm, up), (down_hbm, down))
        )
    ]

    barrier = pltpu.get_barrier_semaphore()

    def greet(lat_at, shift):
        pl.semaphore_signal(barrier, inc=1, device_id=place(lat_at, shift), device_id_type=MESH)

    for step in range(1, n_lat):
        greet((lat + step) % n_lat, 0)
    for shift in (-1, 1):
        greet(lat, shift)

        @pl.when(lat > 0)
        def _():
            greet(lat - 1, shift)

        @pl.when(lat < n_lat - 1)
        def _():
            greet(lat + 1, shift)

    @pl.when(lat == 0)
    def _():
        for other in range(n_lat):
            greet(other, -1)

    @pl.when(lat == n_lat - 1)
    def _():
        for other in range(n_lat):
            greet(other, 1)

    for copy in copies:
        copy.start()
    cur[0] = atm_ref[...]

    fixed = n_lat - 1 + 2 + 2

    @pl.when((lat > 0) & (lat < n_lat - 1))
    def _():
        pl.semaphore_wait(barrier, fixed + 4)

    @pl.when((lat == 0) | (lat == n_lat - 1))
    def _():
        pl.semaphore_wait(barrier, fixed + 2)

    def halo(b, m, index):
        dy, dx = SIDES[index]
        source = cur.at[b, m]
        if dy == 0:
            first = 0 if dx < 0 else length - EDGE
            source = source.at[:, pl.ds(first, EDGE)]
            target = hcol.at[b, m, (1 - dx) // 2]
        elif dx == 0:
            source = source.at[0 if dy < 0 else rows - 1]
            target = hrow.at[b, m, (1 - dy) // 2]
        else:
            first = 0 if dx < 0 else length - EDGE
            source = source.at[0 if dy < 0 else rows - 1, pl.ds(first, EDGE)]
            target = hcor.at[b, m, 1 - dy + (1 - dx) // 2]
        return pltpu.make_async_remote_copy(
            src_ref=source,
            dst_ref=target,
            send_sem=hsend.at[b, m, index],
            recv_sem=hrecv.at[b, m, index],
            device_id=place(lat + dy, dx),
            device_id_type=MESH,
        )

    def each_halo(b, m, act_on, receive):
        for index, (dy, dx) in enumerate(SIDES):
            sign = -dy if receive else dy
            if sign < 0:

                @pl.when(lat > 0)
                def _():
                    act_on(halo(b, m, index))
            elif sign > 0:

                @pl.when(lat < n_lat - 1)
                def _():
                    act_on(halo(b, m, index))
            else:
                act_on(halo(b, m, index))

    for m in range(members):
        each_halo(0, m, lambda copy: copy.start(), False)

    pad[0] = jnp.zeros(pad.shape[1:], F32)
    pad[rows + 1] = jnp.zeros(pad.shape[1:], F32)
    opad[...] = jnp.zeros(opad.shape, F32)
    cpad[...] = jnp.zeros(cpad.shape, F32)
    startpad[...] = jnp.zeros(startpad.shape, F32)
    for r in range(rows):
        row = jnp.broadcast_to(ids_ref[r : r + 1, :].astype(F32), (length, length))
        same[r] = (row == row.T).astype(F32)
        row = jnp.broadcast_to(sea_ref[r : r + 1, :].astype(F32), (length, length))
        seab[r * length : (r + 1) * length] = row.T
    head_row = lax.broadcasted_iota(jnp.int32, (LANES, LANES), 0) // HEAD
    head_col = lax.broadcasted_iota(jnp.int32, (LANES, LANES), 1) // HEAD
    head_mean = jnp.where(head_row == head_col, 1.0 / HEAD, 0.0).astype(BF16)

    def piece_copy(m, step):
        to = (lat + step) % n_lat
        return pltpu.make_async_remote_copy(
            src_ref=senda.at[m, to],
            dst_ref=recva.at[m, lat],
            send_sem=asend.at[m, step],
            recv_sem=arecv.at[m, step],
            device_id=place(to, 0),
            device_id_type=MESH,
        )

    def edge_copy(m, side):
        return pltpu.make_async_remote_copy(
            src_ref=edges.at[m, side],
            dst_ref=edger.at[m, lat],
            send_sem=esend.at[m, side],
            recv_sem=erecv.at[m, lat],
            device_id=place(n_lat - 1, -1) if side == 0 else place(0, 1),
            device_id_type=MESH,
        )

    def edge_landed(m, origin):
        return pltpu.make_async_remote_copy(
            src_ref=edges.at[m, 0],
            dst_ref=edger.at[m, origin],
            send_sem=esend.at[m, 0],
            recv_sem=erecv.at[m, origin],
            device_id=place(n_lat - 1, -1),
            device_id_type=MESH,
        )

    def back_copy(m, step):
        to = (lat + step) % n_lat
        return pltpu.make_async_remote_copy(
            src_ref=sendb.at[m, to],
            dst_ref=recvb.at[m, lat],
            send_sem=bsend.at[m, step],
            recv_sem=brecv.at[m, step],
            device_id=place(to, 0),
            device_id_type=MESH,
        )

    def atmosphere(t, carry):
        b = t // members
        m = t % members
        each_halo(b, m, lambda copy: copy.wait_recv(), True)
        pad[1 : rows + 1, RIM : RIM + length] = cur[b, m].astype(F32)
        pad[1 : rows + 1, :RIM] = hcol[b, m, 0].astype(F32)[:, EDGE - RIM :]
        pad[1 : rows + 1, RIM + length :] = hcol[b, m, 1].astype(F32)[:, :RIM]
        for side, at in ((0, 0), (1, rows + 1)):

            @pl.when((lat > 0) if side == 0 else (lat < n_lat - 1))
            def _():
                pad[at, RIM : RIM + length] = hrow[b, m, side].astype(F32)
                pad[at, :RIM] = hcor[b, m, 2 * side].astype(F32)[EDGE - RIM :]
                pad[at, RIM + length :] = hcor[b, m, 2 * side + 1].astype(F32)[:RIM]

        for r in range(rows):
            for c in range(chunks):
                cols = slice(c * LANES, (c + 1) * LANES)
                total = pad[1 + r, RIM : RIM + length, cols]
                for dy in range(3):
                    for dx in range(3):
                        at = RIM - 1 + dx
                        total = (
                            total
                            + pad[r + dy, at : at + length, cols]
                            * conv_ref[b, dy, dx : dx + 1, cols]
                        )
                mixed[r * length : (r + 1) * length, cols] = total.astype(BF16).astype(F32)

        @pl.when(t == 0)
        def _():
            for copy in copies:
                copy.wait()

        normed = layer_norm(mixed[...], attn_gain_ref[pl.ds(b, 1), :]).astype(BF16)
        for c in range(chunks):
            parts = []
            for which in range(3):
                first = which * width + c * LANES
                parts.append(dot(normed, qkv[b, :, first : first + LANES]))
            query = unit(parts[0], head_mean)
            key = unit(parts[1], head_mean)
            value = parts[2].astype(BF16)
            for r in range(rows):
                own = slice(r * length, (r + 1) * length)
                attended[own, c * LANES : (c + 1) * LANES] = attend_pair(
                    query[own],
                    key[own],
                    value[own],
                    same[r],
                    scales_ref[b, 2 * c],
                    scales_ref[b, 2 * c + 1],
                )
        after = (mixed[...] + dot(attended[...], outw[b])).astype(BF16).astype(F32)
        scaled = (
            layer_norm(after, mlp_gain_ref[pl.ds(b, 1), :]) * min_ref[b, pl.ds(m, 1), :]
        ).astype(BF16)
        total = after
        block = 2 * LANES
        for first in range(0, hidden, block):
            lifted = dot(scaled, up[b, :, first : first + block])
            lifted = lifted * mout_ref[b, pl.ds(m, 1), first : first + block]
            total = total + dot(gelu(lifted).astype(BF16), down[b, first : first + block, :])
        result = total.astype(BF16)
        cur[b + 1, m] = result.reshape(rows, length, width)

        @pl.when(b < blocks - 1)
        def _():
            each_halo(b + 1, m, lambda copy: copy.start(), False)

        @pl.when(b == blocks - 1)
        def _():
            final = cur[blocks, m].reshape(cells, width)
            flux = dot(final, flux_ref[...])
            before = prev_ref[m].reshape(cells, LANES).astype(F32)
            begun = (seab[...] * (before + flux)).astype(BF16)
            start[m] = begun
            wide = begun.astype(F32)
            for r in range(rows):
                startpad[r, RIM : RIM + length] = wide[r * length : (r + 1) * length]
                for to in range(n_lat):
                    senda[m, to, r] = startpad[r, to * piece : to * piece + win].astype(BF16)
                edges[m, 0, r] = begun[r * length : r * length + EDGE]
                edges[m, 1, r] = begun[(r + 1) * length - EDGE : (r + 1) * length]
            for step in range(1, n_lat):
                piece_copy(m, step).start()
            for side in range(2):
                edge_copy(m, side).start()
            recva[m, lat] = senda[m, lat]

        return carry

    lax.fori_loop(0, blocks * members, atmosphere, 0)

    fine_cells = lats * win
    half = win // 2
    coarse_cells = fine_cells // 4

    def coarse_of(index):
        return (index // win) // 2 * half + (index % win) // 2

    def nine_taps(ref, which, count, first, wide):
        total = jnp.zeros((count, wide, LANES), F32)
        for dy in range(3):
            for dx in range(3):
                at = first - 1 + dx
                total = (
                    total
                    + ref[dy : dy + count, at : at + wide]
                    * oconv_ref[which, dy, dx : dx + 1, :][None]
                )
        return total.astype(BF16).reshape(count * wide, LANES)

    def ocean(m, carry):
        for step in range(1, n_lat):
            piece_copy(m, step).wait_recv()
        opad[1 : lats + 1, RIM : RIM + win] = (
            recva[m].astype(F32).reshape(lats, win, LANES)
        )

        @pl.when(lat == 0)
        def _():
            for origin in range(n_lat):
                edge_landed(m, origin).wait_recv()
            west = edger[m].astype(F32).reshape(lats, EDGE, LANES)
            opad[1 : lats + 1, RIM : 2 * RIM] = west[:, EDGE - RIM :]

        @pl.when(lat == n_lat - 1)
        def _():
            for origin in range(n_lat):
                edge_landed(m, origin).wait_recv()
            east = edger[m].astype(F32).reshape(lats, EDGE, LANES)
            opad[1 : lats + 1, 2 * RIM + piece : 3 * RIM + piece] = east[:, :RIM]

        first = gelu(dot(nine_taps(opad, 0, lats, RIM, win), point_ref[0])).astype(BF16)
        fine[...] = first
        to_coarse = coarse_of(lax.broadcasted_iota(jnp.int32, (coarse_cells, fine_cells), 1))
        own = lax.broadcasted_iota(jnp.int32, (coarse_cells, fine_cells), 0)
        pooling = jnp.where(to_coarse == own, 0.25, 0.0).astype(BF16)
        pooled = dot(pooling, first).astype(BF16).astype(F32)
        cpad[1 : lats // 2 + 1, RIM : RIM + half] = pooled.reshape(lats // 2, half, LANES)
        second = nine_taps(cpad, 1, lats // 2, RIM, half)
        coarse = gelu(dot(second, point_ref[1])).astype(BF16)
        wide = coarse.astype(F32)
        normed = layer_norm(wide, ogain_ref[...]).astype(BF16)
        projected = dot(normed, oqkv_ref[...])
        column = lax.broadcasted_iota(jnp.int32, (coarse_cells, coarse_cells), 0) % half
        other = lax.broadcasted_iota(jnp.int32, (coarse_cells, coarse_cells), 1) % half
        seen = attend_pair(
            unit(projected[:, :LANES], head_mean),
            unit(projected[:, LANES : 2 * LANES], head_mean),
            projected[:, 2 * LANES :].astype(BF16),
            (column == other).astype(F32),
            oscale_ref[0],
            oscale_ref[1],
        )
        coarse_next = (wide + dot(seen, oout_ref[...])).astype(BF16)
        from_fine = coarse_of(lax.broadcasted_iota(jnp.int32, (fine_cells, coarse_cells), 0))
        own = lax.broadcasted_iota(jnp.int32, (fine_cells, coarse_cells), 1)
        spread = jnp.where(from_fine == own, 1.0, 0.0).astype(BF16)
        merged = (fine[...].astype(F32) + dot(spread, coarse_next)).astype(BF16).astype(F32)
        opad[1 : lats + 1, RIM : RIM + win] = merged.reshape(lats, win, LANES)
        sendb[m] = nine_taps(opad, 2, lats, 2 * RIM, piece).reshape(sendb.shape[1:])
        for step in range(1, n_lat):
            back_copy(m, step).start()
        recvb[m, lat] = sendb[m, lat]
        return carry

    lax.fori_loop(0, members, ocean, 0)

    def finish(m, carry):
        for step in range(1, n_lat):
            back_copy(m, step).wait_recv()
        for origin in range(n_lat):
            landed = recvb[m, origin].astype(F32)
            for r in range(rows):
                at = r * length + origin * piece
                act[at : at + piece] = landed[r * piece : (r + 1) * piece]
        lifted = gelu(dot(act[...].astype(BF16), point_ref[2]))
        sea = seab[...]
        updated = (sea * (start[m].astype(F32) + lifted)).astype(BF16)
        seaside_ref[m] = updated.reshape(rows, length, LANES)
        back = dot(updated, return_ref[...])
        for c in range(chunks):
            cols = slice(c * LANES, (c + 1) * LANES)
            final = cur[blocks, m, :, :, cols].astype(F32).reshape(cells, LANES)
            air = (final + sea * back[:, cols]).astype(BF16)
            air_ref[m, :, :, cols] = air.reshape(rows, length, LANES)
        for step in range(1, n_lat):
            piece_copy(m, step).wait_send()
            back_copy(m, step).wait_send()
        for side in range(2):
            edge_copy(m, side).wait_send()
        for b in range(blocks):
            each_halo(b, m, lambda copy: copy.wait_send(), False)
        return carry

    lax.fori_loop(0, members, finish, 0)


def per_device(sizes, *args):
    atm, prev = args[0], args[1]
    members, rows, length, width = atm.shape
    channels = prev.shape[-1]
    blocks = args[4].shape[0]
    hidden = args[12].shape[2]
    n_lat = sizes[0]
    piece = length // n_lat
    win = -(-(piece + 2 * RIM) // 16) * 16
    lats = rows * n_lat
    args = list(args)
    args[17] = args[17].reshape(1, channels)
    vmem = pl.BlockSpec(memory_space=pltpu.VMEM)
    smem = pl.BlockSpec(memory_space=pltpu.SMEM)
    hbm = pl.BlockSpec(memory_space=pl.ANY)
    specs = [vmem] * len(args)
    for index in (7, 19):
        specs[index] = smem
    for index in (6, 8, 12, 13):
        specs[index] = hbm
    dma = pltpu.SemaphoreType.DMA
    return pl.pallas_call(
        functools.partial(kernel, sizes),
        out_shape=(
            jax.ShapeDtypeStruct(atm.shape, BF16),
            jax.ShapeDtypeStruct(prev.shape, BF16),
        ),
        in_specs=specs,
        out_specs=(vmem, vmem),
        scratch_shapes=[
            pltpu.VMEM(args[6].shape, BF16),
            pltpu.VMEM(args[8].shape, BF16),
            pltpu.VMEM(args[12].shape, BF16),
            pltpu.VMEM(args[13].shape, BF16),
            pltpu.VMEM((blocks + 1,) + atm.shape, BF16),
            pltpu.VMEM((blocks, members, 2, length, width), BF16),
            pltpu.VMEM((blocks, members, 2, rows, EDGE, width), BF16),
            pltpu.VMEM((blocks, members, 4, EDGE, width), BF16),
            pltpu.VMEM((rows + 2, length + 2 * RIM, width), F32),
            pltpu.VMEM((rows * length, width), F32),
            pltpu.VMEM((rows * length, width), BF16),
            pltpu.VMEM((rows, length, length), F32),
            pltpu.VMEM((rows * length, channels), F32),
            pltpu.VMEM((members, rows * length, channels), BF16),
            pltpu.VMEM((rows, length + win, channels), F32),
            pltpu.VMEM((members, n_lat, rows, win, channels), BF16),
            pltpu.VMEM((members, n_lat, rows, win, channels), BF16),
            pltpu.VMEM((members, 2, rows, EDGE, channels), BF16),
            pltpu.VMEM((members, n_lat, rows, EDGE, channels), BF16),
            pltpu.VMEM((lats + 2, win + 2 * RIM, channels), F32),
            pltpu.VMEM((lats // 2 + 2, win // 2 + 2 * RIM, channels), F32),
            pltpu.VMEM((lats * win, channels), BF16),
            pltpu.VMEM((members, n_lat, rows * piece, channels), BF16),
            pltpu.VMEM((members, n_lat, rows * piece, channels), BF16),
            pltpu.VMEM((rows * length, channels), F32),
            dma((4,)),
            dma((blocks, members, len(SIDES))),
            dma((blocks, members, len(SIDES))),
            dma((members, n_lat)),
            dma((members, n_lat)),
            dma((members, 2)),
            dma((members, n_lat)),
            dma((members, n_lat)),
            dma((members, n_lat)),
        ],
        compiler_params=pltpu.CompilerParams(
            collective_id=0, has_side_effects=True, vmem_limit_bytes=48 * 2**20
        ),
        cost_estimate=pl.CostEstimate(
            flops=4 * 10**9, bytes_accessed=10**7, transcendentals=2 * 10**6
        ),
    )(*args)


def solution(mesh):
    sizes = tuple(mesh.shape[axis] for axis in ("lat", "lon", "comp"))
    field = P(None, "lat", ("lon", "comp"), None)
    plane = P("lat", ("lon", "comp"))
    return jax.shard_map(
        functools.partial(per_device, sizes),
        mesh=mesh,
        in_specs=(field, field, plane, plane) + (P(),) * 18,
        out_specs=(field, field),
        check_vma=False,
    )
```

```python
import functools

import jax
import jax.numpy as jnp
from jax import lax
from jax.experimental import pallas as pl
from jax.experimental.pallas import tpu as pltpu
from jax.sharding import PartitionSpec as P

NORM_EPS = 1e-05
UNIT_EPS = 1e-06
HEAD = 64
LANES = 128
RIM = 8
EDGE = 16
LOG2E = 1.4426950408889634
MESH = pl.DeviceIdType.MESH
F32 = jnp.float32
BF16 = jnp.bfloat16
SIDES = [(dy, dx) for dy in (-1, 0, 1) for dx in (-1, 0, 1) if (dy, dx) != (0, 0)]


TANH_TERMS = (
    7.97884216e-01,
    3.63342834e-02,
    -3.31299374e-05,
    -5.52401755e-05,
    3.96911181e-06,
    -1.33446555e-07,
    1.80561970e-09,
)


def gelu(x):
    square = jnp.minimum(x * x, 36.0)
    inner = TANH_TERMS[-1]
    for term in TANH_TERMS[-2::-1]:
        inner = inner * square + term
    half = 0.5 * x
    return half + half * jnp.tanh(x * inner)


def layer_norm(x, gain):
    centred = x - jnp.mean(x, axis=-1, keepdims=True)
    spread = jnp.mean(centred * centred, axis=-1, keepdims=True)
    return centred * lax.rsqrt(spread + NORM_EPS) * gain


def dot(a, b):
    return jnp.dot(a, b, preferred_element_type=F32)


def unit(p, head_mean):
    mean_square = dot((p * p).astype(BF16), head_mean)
    return (p * lax.rsqrt(mean_square + UNIT_EPS)).astype(BF16)


def attend_pair(q, k, v, mask, scale_a, scale_b):
    n = q.shape[0]
    lane = lax.broadcasted_iota(jnp.int32, (1, LANES), 1)
    low = (lane < HEAD).astype(F32).astype(BF16)
    high = (lane >= HEAD).astype(F32).astype(BF16)
    keys = jnp.concatenate([k * low, k * high], axis=0)
    scores = lax.dot_general(q, keys, (((1,), (1,)), ((), ())), preferred_element_type=F32)
    both = lax.broadcasted_iota(jnp.int32, (1, 2 * n), 1)
    factor = jnp.where(both < n, scale_a, scale_b) * (LOG2E / HEAD)
    terms = jnp.exp2(scores * factor) * jnp.concatenate([mask, mask], axis=1)
    values = jnp.concatenate([v * low, v * high], axis=0)
    ones = jnp.concatenate(
        [jnp.broadcast_to(low, (n, LANES)), jnp.broadcast_to(high, (n, LANES))], axis=0
    )
    result = dot(terms.astype(BF16), jnp.concatenate([values, ones], axis=1))
    return (result[:, :LANES] / result[:, LANES:]).astype(BF16)


def kernel(
    sizes,
    atm_hbm,
    prev_hbm,
    sea_hbm,
    ids_hbm,
    conv_hbm,
    attn_gain_hbm,
    qkv_hbm,
    scales_hbm,
    out_hbm,
    mlp_gain_hbm,
    min_hbm,
    mout_hbm,
    up_hbm,
    down_hbm,
    flux_hbm,
    oconv_hbm,
    point_hbm,
    ogain_hbm,
    oqkv_hbm,
    oscale_hbm,
    oout_hbm,
    return_hbm,
    air_ref,
    seaside_ref,
    prev_ref,
    sea_ref,
    ids_ref,
    conv_ref,
    attn_gain_ref,
    qkv,
    scales_ref,
    outw,
    mlp_gain_ref,
    min_ref,
    mout_ref,
    up,
    down,
    flux_ref,
    oconv_ref,
    point_ref,
    ogain_ref,
    oqkv_ref,
    oscale_ref,
    oout_ref,
    return_ref,
    cur,
    hrow,
    hcol,
    hcor,
    pad,
    mixed,
    attended,
    same,
    seab,
    start,
    startpad,
    senda,
    recva,
    edges,
    edger,
    opad,
    cpad,
    fine,
    sendb,
    recvb,
    act,
    pooling,
    spread,
    osame,
    wsem,
    hsend,
    hrecv,
    asend,
    arecv,
    esend,
    erecv,
    bsend,
    brecv,
):
    n_lat, n_lon, n_comp = sizes
    members, rows, length, width = atm_hbm.shape
    blocks = conv_ref.shape[2]
    hidden = up.shape[2]
    piece = length // n_lat
    win = senda.shape[3]
    lats = n_lat * rows
    cells = rows * length
    chunks = width // LANES
    sectors = n_lon * n_comp
    lat = lax.axis_index("lat")
    sector = lax.axis_index("lon") * n_comp + lax.axis_index("comp")

    def place(lat_at, shift):
        at = (sector + shift + sectors) % sectors
        return {"lat": lat_at, "lon": at // n_comp, "comp": at % n_comp}

    pairs = (
        (atm_hbm, cur.at[0]),
        (sea_hbm, sea_ref),
        (ids_hbm, ids_ref),
        (conv_hbm, conv_ref),
        (prev_hbm, prev_ref),
        (attn_gain_hbm, attn_gain_ref),
        (qkv_hbm, qkv),
        (scales_hbm, scales_ref),
        (out_hbm, outw),
        (mlp_gain_hbm, mlp_gain_ref),
        (min_hbm, min_ref),
        (mout_hbm, mout_ref),
        (up_hbm, up),
        (down_hbm, down),
        (flux_hbm, flux_ref),
        (oconv_hbm, oconv_ref),
        (point_hbm, point_ref),
        (ogain_hbm, ogain_ref),
        (oqkv_hbm, oqkv_ref),
        (oscale_hbm, oscale_ref),
        (oout_hbm, oout_ref),
        (return_hbm, return_ref),
    )
    copies = [
        pltpu.make_async_copy(source, target, wsem.at[i])
        for i, (source, target) in enumerate(pairs)
    ]
    early = 4
    for copy in copies[:early]:
        copy.start()

    barrier = pltpu.get_barrier_semaphore()

    def greet(lat_at, shift):
        pl.semaphore_signal(barrier, inc=1, device_id=place(lat_at, shift), device_id_type=MESH)

    for step in range(1, n_lat):
        greet((lat + step) % n_lat, 0)
    for shift in (-1, 1):
        greet(lat, shift)

        @pl.when(lat > 0)
        def _():
            greet(lat - 1, shift)

        @pl.when(lat < n_lat - 1)
        def _():
            greet(lat + 1, shift)

    @pl.when(lat == 0)
    def _():
        for other in range(n_lat):
            greet(other, -1)

    @pl.when(lat == n_lat - 1)
    def _():
        for other in range(n_lat):
            greet(other, 1)


    fixed = n_lat - 1 + 2 + 2

    @pl.when((lat > 0) & (lat < n_lat - 1))
    def _():
        pl.semaphore_wait(barrier, fixed + 4)

    @pl.when((lat == 0) | (lat == n_lat - 1))
    def _():
        pl.semaphore_wait(barrier, fixed + 2)

    def halo(b, m, index):
        dy, dx = SIDES[index]
        source = cur.at[b, m]
        if dy == 0:
            first = 0 if dx < 0 else length - EDGE
            source = source.at[:, pl.ds(first, EDGE)]
            target = hcol.at[b, m, (1 - dx) // 2]
        elif dx == 0:
            source = source.at[0 if dy < 0 else rows - 1]
            target = hrow.at[b, m, (1 - dy) // 2]
        else:
            first = 0 if dx < 0 else length - EDGE
            source = source.at[0 if dy < 0 else rows - 1, pl.ds(first, EDGE)]
            target = hcor.at[b, m, 1 - dy + (1 - dx) // 2]
        return pltpu.make_async_remote_copy(
            src_ref=source,
            dst_ref=target,
            send_sem=hsend.at[b, m, index],
            recv_sem=hrecv.at[b, m, index],
            device_id=place(lat + dy, dx),
            device_id_type=MESH,
        )

    def each_halo(b, m, act_on, receive):
        for index, (dy, dx) in enumerate(SIDES):
            sign = -dy if receive else dy
            if sign < 0:

                @pl.when(lat > 0)
                def _():
                    act_on(halo(b, m, index))
            elif sign > 0:

                @pl.when(lat < n_lat - 1)
                def _():
                    act_on(halo(b, m, index))
            else:
                act_on(halo(b, m, index))

    copies[0].wait()
    each_halo(0, 0, lambda copy: copy.start(), False)
    for copy in copies[early:]:
        copy.start()
    for copy in copies[1:early]:
        copy.wait()

    pad[0] = jnp.zeros(pad.shape[1:], F32)
    pad[rows + 1] = jnp.zeros(pad.shape[1:], F32)
    opad[...] = jnp.zeros(opad.shape, F32)
    cpad[...] = jnp.zeros(cpad.shape, F32)
    startpad[...] = jnp.zeros(startpad.shape, F32)
    for r in range(rows):
        row = jnp.broadcast_to(ids_ref[r : r + 1, :].astype(F32), (length, length))
        same[r] = (row == row.T).astype(F32)
        row = jnp.broadcast_to(sea_ref[r : r + 1, :].astype(F32), (length, length))
        seab[r * length : (r + 1) * length] = row.T
    head_row = lax.broadcasted_iota(jnp.int32, (LANES, LANES), 0) // HEAD
    head_col = lax.broadcasted_iota(jnp.int32, (LANES, LANES), 1) // HEAD
    head_mean = jnp.where(head_row == head_col, 1.0 / HEAD, 0.0).astype(BF16)

    fine_cells = lats * win
    half = win // 2
    coarse_cells = fine_cells // 4
    index = lax.broadcasted_iota(jnp.int32, (1, fine_cells), 1)
    to_coarse = (index // win) // 2 * half + (index % win) // 2
    own = lax.broadcasted_iota(jnp.int32, (coarse_cells, 1), 0)
    member_of = jnp.where(own == to_coarse, 1.0, 0.0)
    pooling[...] = (0.25 * member_of).astype(BF16)
    spread[...] = member_of.T.astype(BF16)
    index = lax.broadcasted_iota(jnp.int32, (1, coarse_cells), 1) % half
    row = jnp.broadcast_to(index.astype(F32), (coarse_cells, coarse_cells))
    osame[...] = (row == row.T).astype(F32)

    def piece_copy(m, step):
        to = (lat + step) % n_lat
        return pltpu.make_async_remote_copy(
            src_ref=senda.at[m, to],
            dst_ref=recva.at[m, lat],
            send_sem=asend.at[m, step],
            recv_sem=arecv.at[m, step],
            device_id=place(to, 0),
            device_id_type=MESH,
        )

    def edge_copy(m, side):
        return pltpu.make_async_remote_copy(
            src_ref=edges.at[m, side],
            dst_ref=edger.at[m, lat],
            send_sem=esend.at[m, side],
            recv_sem=erecv.at[m, lat],
            device_id=place(n_lat - 1, -1) if side == 0 else place(0, 1),
            device_id_type=MESH,
        )

    def edge_landed(m, origin):
        return pltpu.make_async_remote_copy(
            src_ref=edges.at[m, 0],
            dst_ref=edger.at[m, origin],
            send_sem=esend.at[m, 0],
            recv_sem=erecv.at[m, origin],
            device_id=place(n_lat - 1, -1),
            device_id_type=MESH,
        )

    def back_copy(m, step):
        to = (lat + step) % n_lat
        return pltpu.make_async_remote_copy(
            src_ref=sendb.at[m, to],
            dst_ref=recvb.at[m, lat],
            send_sem=bsend.at[m, step],
            recv_sem=brecv.at[m, step],
            device_id=place(to, 0),
            device_id_type=MESH,
        )

    def atmosphere(t, carry):
        b = t // members
        m = t % members
        each_halo(b, m, lambda copy: copy.wait_recv(), True)

        @pl.when(t + 1 < members)
        def _():
            each_halo(0, t + 1, lambda copy: copy.start(), False)

        pad[1 : rows + 1, RIM : RIM + length] = cur[b, m].astype(F32)
        pad[1 : rows + 1, :RIM] = hcol[b, m, 0].astype(F32)[:, EDGE - RIM :]
        pad[1 : rows + 1, RIM + length :] = hcol[b, m, 1].astype(F32)[:, :RIM]
        for side, at in ((0, 0), (1, rows + 1)):

            @pl.when((lat > 0) if side == 0 else (lat < n_lat - 1))
            def _():
                pad[at, RIM : RIM + length] = hrow[b, m, side].astype(F32)
                pad[at, :RIM] = hcor[b, m, 2 * side].astype(F32)[EDGE - RIM :]
                pad[at, RIM + length :] = hcor[b, m, 2 * side + 1].astype(F32)[:RIM]

        taps = [[conv_ref[dy, dx, pl.ds(b, 1), :] for dx in range(3)] for dy in range(3)]
        for r in range(rows):
            for c in range(chunks):
                cols = slice(c * LANES, (c + 1) * LANES)
                total = pad[1 + r, RIM : RIM + length, cols]
                for dy in range(3):
                    for dx in range(3):
                        at = RIM - 1 + dx
                        total = (
                            total
                            + pad[r + dy, at : at + length, cols]
                            * taps[dy][dx][:, cols]
                        )
                mixed[r * length : (r + 1) * length, cols] = total.astype(BF16).astype(F32)

        @pl.when(t == 0)
        def _():
            for copy in copies[early:]:
                copy.wait()

        normed = layer_norm(mixed[...], attn_gain_ref[pl.ds(b, 1), :]).astype(BF16)
        projected = dot(normed, qkv[b])
        for c in range(chunks):
            parts = []
            for which in range(3):
                first = which * width + c * LANES
                parts.append(projected[:, first : first + LANES])
            query = unit(parts[0], head_mean)
            key = unit(parts[1], head_mean)
            value = parts[2].astype(BF16)
            for r in range(rows):
                own = slice(r * length, (r + 1) * length)
                attended[own, c * LANES : (c + 1) * LANES] = attend_pair(
                    query[own],
                    key[own],
                    value[own],
                    same[r],
                    scales_ref[b, 2 * c],
                    scales_ref[b, 2 * c + 1],
                )
        after = (mixed[...] + dot(attended[...], outw[b])).astype(BF16).astype(F32)
        scaled = (
            layer_norm(after, mlp_gain_ref[pl.ds(b, 1), :]) * min_ref[b, pl.ds(m, 1), :]
        ).astype(BF16)
        total = after
        block = 2 * LANES
        for first in range(0, hidden, block):
            lifted = dot(scaled, up[b, :, first : first + block])
            lifted = lifted * mout_ref[b, pl.ds(m, 1), first : first + block]
            total = total + dot(gelu(lifted).astype(BF16), down[b, first : first + block, :])
        result = total.astype(BF16)
        cur[b + 1, m] = result.reshape(rows, length, width)

        @pl.when(b < blocks - 1)
        def _():
            each_halo(b + 1, m, lambda copy: copy.start(), False)

        @pl.when(b == blocks - 1)
        def _():
            final = cur[blocks, m].reshape(cells, width)
            flux = dot(final, flux_ref[...])
            before = prev_ref[m].reshape(cells, LANES).astype(F32)
            begun = (seab[...] * (before + flux)).astype(BF16)
            start[m] = begun
            wide = begun.astype(F32)
            for r in range(rows):
                startpad[r, RIM : RIM + length] = wide[r * length : (r + 1) * length]
                for to in range(n_lat):
                    senda[m, to, r] = startpad[r, to * piece : to * piece + win].astype(BF16)
                edges[m, 0, r] = begun[r * length : r * length + EDGE]
                edges[m, 1, r] = begun[(r + 1) * length - EDGE : (r + 1) * length]
            for step in range(1, n_lat):
                piece_copy(m, step).start()
            for side in range(2):
                edge_copy(m, side).start()
            recva[m, lat] = senda[m, lat]

        return carry

    lax.fori_loop(0, blocks * members, atmosphere, 0)

    def nine_taps(ref, which, count, first, wide):
        group = max(1, 128 // wide)
        parts = []
        for top in range(0, count, group):
            size = min(group, count - top)
            total = None
            for dy in range(3):
                for dx in range(3):
                    at = first - 1 + dx
                    term = (
                        ref[top + dy : top + dy + size, at : at + wide]
                        * oconv_ref[which, dy, dx : dx + 1, :][None]
                    )
                    total = term if total is None else total + term
            parts.append(total.astype(BF16).reshape(size * wide, LANES))
        return jnp.concatenate(parts, axis=0)

    def ocean(m, carry):
        for step in range(1, n_lat):
            piece_copy(m, step).wait_recv()
        opad[1 : lats + 1, RIM : RIM + win] = (
            recva[m].astype(F32).reshape(lats, win, LANES)
        )

        @pl.when(lat == 0)
        def _():
            for origin in range(n_lat):
                edge_landed(m, origin).wait_recv()
            west = edger[m].astype(F32).reshape(lats, EDGE, LANES)
            opad[1 : lats + 1, RIM : 2 * RIM] = west[:, EDGE - RIM :]

        @pl.when(lat == n_lat - 1)
        def _():
            for origin in range(n_lat):
                edge_landed(m, origin).wait_recv()
            east = edger[m].astype(F32).reshape(lats, EDGE, LANES)
            opad[1 : lats + 1, 2 * RIM + piece : 3 * RIM + piece] = east[:, :RIM]

        first = gelu(dot(nine_taps(opad, 0, lats, RIM, win), point_ref[0])).astype(BF16)
        fine[...] = first
        pooled = dot(pooling[...], first).astype(BF16).astype(F32)
        cpad[1 : lats // 2 + 1, RIM : RIM + half] = pooled.reshape(lats // 2, half, LANES)
        second = nine_taps(cpad, 1, lats // 2, RIM, half)
        coarse = gelu(dot(second, point_ref[1])).astype(BF16)
        wide = coarse.astype(F32)
        normed = layer_norm(wide, ogain_ref[...]).astype(BF16)
        projected = dot(normed, oqkv_ref[...])
        seen = attend_pair(
            unit(projected[:, :LANES], head_mean),
            unit(projected[:, LANES : 2 * LANES], head_mean),
            projected[:, 2 * LANES :].astype(BF16),
            osame[...],
            oscale_ref[0],
            oscale_ref[1],
        )
        coarse_next = (wide + dot(seen, oout_ref[...])).astype(BF16)
        merged = (fine[...].astype(F32) + dot(spread[...], coarse_next)).astype(BF16).astype(F32)
        opad[1 : lats + 1, RIM : RIM + win] = merged.reshape(lats, win, LANES)
        sendb[m] = nine_taps(opad, 2, lats, 2 * RIM, piece).reshape(sendb.shape[1:])
        for step in range(1, n_lat):
            back_copy(m, step).start()
        recvb[m, lat] = sendb[m, lat]
        return carry

    lax.fori_loop(0, members, ocean, 0)

    def finish(m, carry):
        for step in range(1, n_lat):
            back_copy(m, step).wait_recv()
        for origin in range(n_lat):
            landed = recvb[m, origin].astype(F32)
            for r in range(rows):
                at = r * length + origin * piece
                act[at : at + piece] = landed[r * piece : (r + 1) * piece]
        lifted = gelu(dot(act[...].astype(BF16), point_ref[2]))
        sea = seab[...]
        updated = (sea * (start[m].astype(F32) + lifted)).astype(BF16)
        seaside_ref[m] = updated.reshape(rows, length, LANES)
        back = dot(updated, return_ref[...])
        for c in range(chunks):
            cols = slice(c * LANES, (c + 1) * LANES)
            final = cur[blocks, m, :, :, cols].astype(F32).reshape(cells, LANES)
            air = (final + sea * back[:, cols]).astype(BF16)
            air_ref[m, :, :, cols] = air.reshape(rows, length, LANES)
        for step in range(1, n_lat):
            piece_copy(m, step).wait_send()
            back_copy(m, step).wait_send()
        for side in range(2):
            edge_copy(m, side).wait_send()
        for b in range(blocks):
            each_halo(b, m, lambda copy: copy.wait_send(), False)
        return carry

    lax.fori_loop(0, members, finish, 0)


def per_device(sizes, *args):
    atm, prev = args[0], args[1]
    members, rows, length, width = atm.shape
    channels = prev.shape[-1]
    blocks = args[4].shape[0]
    hidden = args[12].shape[2]
    n_lat = sizes[0]
    piece = length // n_lat
    win = -(-(piece + 2 * RIM) // 16) * 16
    lats = rows * n_lat
    args = list(args)
    args[17] = args[17].reshape(1, channels)
    args[4] = args[4].transpose(1, 2, 0, 3)
    vmem = pl.BlockSpec(memory_space=pltpu.VMEM)
    specs = [pl.BlockSpec(memory_space=pltpu.HBM)] * len(args)
    kept = [
        (pltpu.SMEM if index in (7, 19) else pltpu.VMEM)(arg.shape, arg.dtype)
        for index, arg in enumerate(args)
    ]
    dma = pltpu.SemaphoreType.DMA
    return pl.pallas_call(
        functools.partial(kernel, sizes),
        out_shape=(
            jax.ShapeDtypeStruct(atm.shape, BF16),
            jax.ShapeDtypeStruct(prev.shape, BF16),
        ),
        in_specs=specs,
        out_specs=(vmem, vmem),
        scratch_shapes=kept[1:]
        + [
            pltpu.VMEM((blocks + 1,) + atm.shape, BF16),
            pltpu.VMEM((blocks, members, 2, length, width), BF16),
            pltpu.VMEM((blocks, members, 2, rows, EDGE, width), BF16),
            pltpu.VMEM((blocks, members, 4, EDGE, width), BF16),
            pltpu.VMEM((rows + 2, length + 2 * RIM, width), F32),
            pltpu.VMEM((rows * length, width), F32),
            pltpu.VMEM((rows * length, width), BF16),
            pltpu.VMEM((rows, length, length), F32),
            pltpu.VMEM((rows * length, channels), F32),
            pltpu.VMEM((members, rows * length, channels), BF16),
            pltpu.VMEM((rows, length + win, channels), F32),
            pltpu.VMEM((members, n_lat, rows, win, channels), BF16),
            pltpu.VMEM((members, n_lat, rows, win, channels), BF16),
            pltpu.VMEM((members, 2, rows, EDGE, channels), BF16),
            pltpu.VMEM((members, n_lat, rows, EDGE, channels), BF16),
            pltpu.VMEM((lats + 2, win + 2 * RIM, channels), F32),
            pltpu.VMEM((lats // 2 + 2, win // 2 + 2 * RIM, channels), F32),
            pltpu.VMEM((lats * win, channels), BF16),
            pltpu.VMEM((members, n_lat, rows * piece, channels), BF16),
            pltpu.VMEM((members, n_lat, rows * piece, channels), BF16),
            pltpu.VMEM((rows * length, channels), F32),
            pltpu.VMEM((lats * win // 4, lats * win), BF16),
            pltpu.VMEM((lats * win, lats * win // 4), BF16),
            pltpu.VMEM((lats * win // 4, lats * win // 4), F32),
            dma((len(args),)),
            dma((blocks, members, len(SIDES))),
            dma((blocks, members, len(SIDES))),
            dma((members, n_lat)),
            dma((members, n_lat)),
            dma((members, 2)),
            dma((members, n_lat)),
            dma((members, n_lat)),
            dma((members, n_lat)),
        ],
        compiler_params=pltpu.CompilerParams(
            collective_id=0, has_side_effects=True, vmem_limit_bytes=48 * 2**20
        ),
        cost_estimate=pl.CostEstimate(
            flops=4 * 10**9, bytes_accessed=10**7, transcendentals=2 * 10**6
        ),
    )(*args)


def solution(mesh):
    sizes = tuple(mesh.shape[axis] for axis in ("lat", "lon", "comp"))
    field = P(None, "lat", ("lon", "comp"), None)
    plane = P("lat", ("lon", "comp"))
    return jax.shard_map(
        functools.partial(per_device, sizes),
        mesh=mesh,
        in_specs=(field, field, plane, plane) + (P(),) * 18,
        out_specs=(field, field),
        check_vma=False,
    )
```

```python
import functools

import jax
import jax.numpy as jnp
from jax import lax
from jax.experimental import pallas as pl
from jax.experimental.pallas import tpu as pltpu
from jax.sharding import PartitionSpec as P

NORM_EPS = 1e-05
UNIT_EPS = 1e-06
HEAD = 64
LANES = 128
RIM = 8
EDGE = 16
LOG2E = 1.4426950408889634
MESH = pl.DeviceIdType.MESH
F32 = jnp.float32
BF16 = jnp.bfloat16
SIDES = [(dy, dx) for dy in (-1, 0, 1) for dx in (-1, 0, 1) if (dy, dx) != (0, 0)]


def gelu(x):
    half = 0.5 * x
    return half + half * lax.erf(x * 0.7071067811865476)


def layer_norm(x, gain):
    centred = x - jnp.mean(x, axis=-1, keepdims=True)
    spread = jnp.mean(centred * centred, axis=-1, keepdims=True)
    return centred * lax.rsqrt(spread + NORM_EPS) * gain


def dot(a, b):
    return jnp.dot(a, b, preferred_element_type=F32)


def unit(p, head_mean):
    mean_square = dot((p * p).astype(BF16), head_mean)
    return (p * lax.rsqrt(mean_square + UNIT_EPS)).astype(BF16)


def attend_pair(q, k, v, mask, scale_a, scale_b):
    n = q.shape[0]
    lane = lax.broadcasted_iota(jnp.int32, (1, LANES), 1)
    low = (lane < HEAD).astype(F32).astype(BF16)
    high = (lane >= HEAD).astype(F32).astype(BF16)
    keys = jnp.concatenate([k * low, k * high], axis=0)
    scores = lax.dot_general(q, keys, (((1,), (1,)), ((), ())), preferred_element_type=F32)
    both = lax.broadcasted_iota(jnp.int32, (1, 2 * n), 1)
    factor = jnp.where(both < n, scale_a, scale_b) * (LOG2E / HEAD)
    terms = jnp.exp2(scores * factor) * jnp.concatenate([mask, mask], axis=1)
    values = jnp.concatenate([v * low, v * high], axis=0)
    ones = jnp.concatenate(
        [jnp.broadcast_to(low, (n, LANES)), jnp.broadcast_to(high, (n, LANES))], axis=0
    )
    result = dot(terms.astype(BF16), jnp.concatenate([values, ones], axis=1))
    return (result[:, :LANES] / result[:, LANES:]).astype(BF16)


def kernel(
    sizes,
    atm_hbm,
    prev_hbm,
    sea_hbm,
    ids_hbm,
    conv_hbm,
    attn_gain_hbm,
    qkv_hbm,
    scales_hbm,
    out_hbm,
    mlp_gain_hbm,
    min_hbm,
    mout_hbm,
    up_hbm,
    down_hbm,
    flux_hbm,
    oconv_hbm,
    point_hbm,
    ogain_hbm,
    oqkv_hbm,
    oscale_hbm,
    oout_hbm,
    return_hbm,
    air_ref,
    seaside_ref,
    prev_ref,
    sea_ref,
    ids_ref,
    conv_ref,
    attn_gain_ref,
    qkv,
    scales_ref,
    outw,
    mlp_gain_ref,
    min_ref,
    mout_ref,
    up,
    down,
    flux_ref,
    oconv_ref,
    point_ref,
    ogain_ref,
    oqkv_ref,
    oscale_ref,
    oout_ref,
    return_ref,
    cur,
    hrow,
    hcol,
    hcor,
    pad,
    mixed,
    attended,
    same,
    seab,
    start,
    startpad,
    senda,
    recva,
    edges,
    edger,
    opad,
    cpad,
    fine,
    sendb,
    recvb,
    act,
    pooling,
    spread,
    osame,
    active,
    wsem,
    hsend,
    hrecv,
    asend,
    arecv,
    esend,
    erecv,
    bsend,
    brecv,
):
    n_lat, n_lon, n_comp = sizes
    members, rows, length, width = atm_hbm.shape
    blocks = conv_ref.shape[2]
    hidden = up.shape[2]
    piece = length // n_lat
    win = senda.shape[3]
    lats = n_lat * rows
    cells = rows * length
    chunks = width // LANES
    sectors = n_lon * n_comp
    lat = lax.axis_index("lat")
    sector = lax.axis_index("lon") * n_comp + lax.axis_index("comp")

    def place(lat_at, shift):
        at = (sector + shift + sectors) % sectors
        return {"lat": lat_at, "lon": at // n_comp, "comp": at % n_comp}

    pairs = (
        (atm_hbm, cur.at[0]),
        (sea_hbm, sea_ref),
        (ids_hbm, ids_ref),
        (conv_hbm, conv_ref),
        (prev_hbm, prev_ref),
        (attn_gain_hbm, attn_gain_ref),
        (qkv_hbm, qkv),
        (scales_hbm, scales_ref),
        (out_hbm, outw),
        (mlp_gain_hbm, mlp_gain_ref),
        (min_hbm, min_ref),
        (mout_hbm, mout_ref),
        (up_hbm, up),
        (down_hbm, down),
        (flux_hbm, flux_ref),
        (oconv_hbm, oconv_ref),
        (point_hbm, point_ref),
        (ogain_hbm, ogain_ref),
        (oqkv_hbm, oqkv_ref),
        (oscale_hbm, oscale_ref),
        (oout_hbm, oout_ref),
        (return_hbm, return_ref),
    )
    copies = [
        pltpu.make_async_copy(source, target, wsem.at[i])
        for i, (source, target) in enumerate(pairs)
    ]
    early = 4
    for copy in copies[:early]:
        copy.start()

    barrier = pltpu.get_barrier_semaphore()

    def greet(lat_at, shift):
        pl.semaphore_signal(barrier, inc=1, device_id=place(lat_at, shift), device_id_type=MESH)

    for step in range(1, n_lat):
        greet((lat + step) % n_lat, 0)
    for shift in (-1, 1):
        greet(lat, shift)

        @pl.when(lat > 0)
        def _():
            greet(lat - 1, shift)

        @pl.when(lat < n_lat - 1)
        def _():
            greet(lat + 1, shift)

    @pl.when(lat == 0)
    def _():
        for other in range(n_lat):
            greet(other, -1)

    @pl.when(lat == n_lat - 1)
    def _():
        for other in range(n_lat):
            greet(other, 1)


    fixed = n_lat - 1 + 2 + 2

    @pl.when((lat > 0) & (lat < n_lat - 1))
    def _():
        pl.semaphore_wait(barrier, fixed + 4)

    @pl.when((lat == 0) | (lat == n_lat - 1))
    def _():
        pl.semaphore_wait(barrier, fixed + 2)

    def halo(b, m, index):
        dy, dx = SIDES[index]
        source = cur.at[b, m]
        if dy == 0:
            first = 0 if dx < 0 else length - EDGE
            source = source.at[:, pl.ds(first, EDGE)]
            target = hcol.at[b, m, (1 - dx) // 2]
        elif dx == 0:
            source = source.at[0 if dy < 0 else rows - 1]
            target = hrow.at[b, m, (1 - dy) // 2]
        else:
            first = 0 if dx < 0 else length - EDGE
            source = source.at[0 if dy < 0 else rows - 1, pl.ds(first, EDGE)]
            target = hcor.at[b, m, 1 - dy + (1 - dx) // 2]
        return pltpu.make_async_remote_copy(
            src_ref=source,
            dst_ref=target,
            send_sem=hsend.at[b, m, index],
            recv_sem=hrecv.at[b, m, index],
            device_id=place(lat + dy, dx),
            device_id_type=MESH,
        )

    def each_halo(b, m, act_on, receive):
        for index, (dy, dx) in enumerate(SIDES):
            sign = -dy if receive else dy
            if sign < 0:

                @pl.when(lat > 0)
                def _():
                    act_on(halo(b, m, index))
            elif sign > 0:

                @pl.when(lat < n_lat - 1)
                def _():
                    act_on(halo(b, m, index))
            else:
                act_on(halo(b, m, index))

    copies[0].wait()
    each_halo(0, 0, lambda copy: copy.start(), False)
    for copy in copies[early:]:
        copy.start()
    for copy in copies[1:early]:
        copy.wait()

    pad[0] = jnp.zeros(pad.shape[1:], F32)
    pad[rows + 1] = jnp.zeros(pad.shape[1:], F32)
    opad[...] = jnp.zeros(opad.shape, F32)
    cpad[...] = jnp.zeros(cpad.shape, F32)
    startpad[...] = jnp.zeros(startpad.shape, F32)
    for r in range(rows):
        row = jnp.broadcast_to(ids_ref[r : r + 1, :].astype(F32), (length, length))
        same[r] = (row == row.T).astype(F32)
        row = jnp.broadcast_to(sea_ref[r : r + 1, :].astype(F32), (length, length))
        seab[r * length : (r + 1) * length] = row.T
    head_row = lax.broadcasted_iota(jnp.int32, (LANES, LANES), 0) // HEAD
    head_col = lax.broadcasted_iota(jnp.int32, (LANES, LANES), 1) // HEAD
    head_mean = jnp.where(head_row == head_col, 1.0 / HEAD, 0.0).astype(BF16)

    fine_cells = lats * win
    half = win // 2
    coarse_cells = fine_cells // 4
    index = lax.broadcasted_iota(jnp.int32, (1, fine_cells), 1)
    to_coarse = (index // win) // 2 * half + (index % win) // 2
    own = lax.broadcasted_iota(jnp.int32, (coarse_cells, 1), 0)
    member_of = jnp.where(own == to_coarse, 1.0, 0.0)
    pooling[...] = (0.25 * member_of).astype(BF16)
    spread[...] = member_of.T.astype(BF16)
    index = lax.broadcasted_iota(jnp.int32, (1, coarse_cells), 1) % half
    row = jnp.broadcast_to(index.astype(F32), (coarse_cells, coarse_cells))
    osame[...] = (row == row.T).astype(F32)

    def piece_copy(m, step):
        to = (lat + step) % n_lat
        return pltpu.make_async_remote_copy(
            src_ref=senda.at[m, to],
            dst_ref=recva.at[m, lat],
            send_sem=asend.at[m, step],
            recv_sem=arecv.at[m, step],
            device_id=place(to, 0),
            device_id_type=MESH,
        )

    def edge_copy(m, side):
        return pltpu.make_async_remote_copy(
            src_ref=edges.at[m, side],
            dst_ref=edger.at[m, lat],
            send_sem=esend.at[m, side],
            recv_sem=erecv.at[m, lat],
            device_id=place(n_lat - 1, -1) if side == 0 else place(0, 1),
            device_id_type=MESH,
        )

    def edge_landed(m, origin):
        return pltpu.make_async_remote_copy(
            src_ref=edges.at[m, 0],
            dst_ref=edger.at[m, origin],
            send_sem=esend.at[m, 0],
            recv_sem=erecv.at[m, origin],
            device_id=place(n_lat - 1, -1),
            device_id_type=MESH,
        )

    def back_copy(m, step):
        to = (lat + step) % n_lat
        return pltpu.make_async_remote_copy(
            src_ref=sendb.at[m, to],
            dst_ref=recvb.at[m, lat],
            send_sem=bsend.at[m, step],
            recv_sem=brecv.at[m, step],
            device_id=place(to, 0),
            device_id_type=MESH,
        )

    def atmosphere(t, carry):
        b = t // members
        m = t % members
        each_halo(b, m, lambda copy: copy.wait_recv(), True)

        @pl.when(t + 1 < members)
        def _():
            each_halo(0, t + 1, lambda copy: copy.start(), False)

        pad[1 : rows + 1, RIM : RIM + length] = cur[b, m].astype(F32)
        pad[1 : rows + 1, :RIM] = hcol[b, m, 0].astype(F32)[:, EDGE - RIM :]
        pad[1 : rows + 1, RIM + length :] = hcol[b, m, 1].astype(F32)[:, :RIM]
        for side, at in ((0, 0), (1, rows + 1)):

            @pl.when((lat > 0) if side == 0 else (lat < n_lat - 1))
            def _():
                pad[at, RIM : RIM + length] = hrow[b, m, side].astype(F32)
                pad[at, :RIM] = hcor[b, m, 2 * side].astype(F32)[EDGE - RIM :]
                pad[at, RIM + length :] = hcor[b, m, 2 * side + 1].astype(F32)[:RIM]

        taps = [[conv_ref[dy, dx, pl.ds(b, 1), :] for dx in range(3)] for dy in range(3)]
        for r in range(rows):
            for c in range(chunks):
                cols = slice(c * LANES, (c + 1) * LANES)
                total = pad[1 + r, RIM : RIM + length, cols]
                for dx in range(3):
                    part = pad[r, :, cols] * taps[0][dx][:, cols]
                    for dy in range(1, 3):
                        part = part + pad[r + dy, :, cols] * taps[dy][dx][:, cols]
                    if dx != 1:
                        part = pltpu.roll(part, (1 - dx) % part.shape[0], 0)
                    total = total + part[RIM : RIM + length]
                mixed[r * length : (r + 1) * length, cols] = total.astype(BF16).astype(F32)

        @pl.when(t == 0)
        def _():
            for copy in copies[early:]:
                copy.wait()

        normed = layer_norm(mixed[...], attn_gain_ref[pl.ds(b, 1), :]).astype(BF16)
        projected = dot(normed, qkv[b])
        for c in range(chunks):
            parts = []
            for which in range(3):
                first = which * width + c * LANES
                parts.append(projected[:, first : first + LANES])
            query = unit(parts[0], head_mean)
            key = unit(parts[1], head_mean)
            value = parts[2].astype(BF16)
            for r in range(rows):
                own = slice(r * length, (r + 1) * length)
                attended[own, c * LANES : (c + 1) * LANES] = attend_pair(
                    query[own],
                    key[own],
                    value[own],
                    same[r],
                    scales_ref[b, 2 * c],
                    scales_ref[b, 2 * c + 1],
                )
        after = (mixed[...] + dot(attended[...], outw[b])).astype(BF16).astype(F32)
        scaled = (
            layer_norm(after, mlp_gain_ref[pl.ds(b, 1), :]) * min_ref[b, pl.ds(m, 1), :]
        ).astype(BF16)
        block = 2 * LANES
        for first in range(0, hidden, block):
            lifted = dot(scaled, up[b, :, first : first + block])
            lifted = lifted * mout_ref[b, pl.ds(m, 1), first : first + block]
            active[:, first : first + block] = gelu(lifted).astype(BF16)
        result = (after + dot(active[...], down[b])).astype(BF16)
        cur[b + 1, m] = result.reshape(rows, length, width)

        @pl.when(b < blocks - 1)
        def _():
            each_halo(b + 1, m, lambda copy: copy.start(), False)

        @pl.when(b == blocks - 1)
        def _():
            final = cur[blocks, m].reshape(cells, width)
            flux = dot(final, flux_ref[...])
            before = prev_ref[m].reshape(cells, LANES).astype(F32)
            begun = (seab[...] * (before + flux)).astype(BF16)
            start[m] = begun
            wide = begun.astype(F32)
            for r in range(rows):
                startpad[r, RIM : RIM + length] = wide[r * length : (r + 1) * length]
                for to in range(n_lat):
                    senda[m, to, r] = startpad[r, to * piece : to * piece + win].astype(BF16)
                edges[m, 0, r] = begun[r * length : r * length + EDGE]
                edges[m, 1, r] = begun[(r + 1) * length - EDGE : (r + 1) * length]
            for step in range(1, n_lat):
                piece_copy(m, step).start()
            for side in range(2):
                edge_copy(m, side).start()
            recva[m, lat] = senda[m, lat]

        return carry

    lax.fori_loop(0, blocks * members, atmosphere, 0)

    def nine_taps(ref, which, count, first, wide):
        group = max(1, 128 // wide)
        parts = []
        for top in range(0, count, group):
            size = min(group, count - top)
            total = None
            for dy in range(3):
                for dx in range(3):
                    at = first - 1 + dx
                    term = (
                        ref[top + dy : top + dy + size, at : at + wide]
                        * oconv_ref[which, dy, dx : dx + 1, :][None]
                    )
                    total = term if total is None else total + term
            parts.append(total.astype(BF16).reshape(size * wide, LANES))
        return jnp.concatenate(parts, axis=0)

    def ocean(m, carry):
        for step in range(1, n_lat):
            piece_copy(m, step).wait_recv()
        opad[1 : lats + 1, RIM : RIM + win] = (
            recva[m].astype(F32).reshape(lats, win, LANES)
        )

        @pl.when(lat == 0)
        def _():
            for origin in range(n_lat):
                edge_landed(m, origin).wait_recv()
            west = edger[m].astype(F32).reshape(lats, EDGE, LANES)
            opad[1 : lats + 1, RIM : 2 * RIM] = west[:, EDGE - RIM :]

        @pl.when(lat == n_lat - 1)
        def _():
            for origin in range(n_lat):
                edge_landed(m, origin).wait_recv()
            east = edger[m].astype(F32).reshape(lats, EDGE, LANES)
            opad[1 : lats + 1, 2 * RIM + piece : 3 * RIM + piece] = east[:, :RIM]

        first = gelu(dot(nine_taps(opad, 0, lats, RIM, win), point_ref[0])).astype(BF16)
        fine[...] = first
        pooled = dot(pooling[...], first).astype(BF16).astype(F32)
        cpad[1 : lats // 2 + 1, RIM : RIM + half] = pooled.reshape(lats // 2, half, LANES)
        second = nine_taps(cpad, 1, lats // 2, RIM, half)
        coarse = gelu(dot(second, point_ref[1])).astype(BF16)
        wide = coarse.astype(F32)
        normed = layer_norm(wide, ogain_ref[...]).astype(BF16)
        projected = dot(normed, oqkv_ref[...])
        seen = attend_pair(
            unit(projected[:, :LANES], head_mean),
            unit(projected[:, LANES : 2 * LANES], head_mean),
            projected[:, 2 * LANES :].astype(BF16),
            osame[...],
            oscale_ref[0],
            oscale_ref[1],
        )
        coarse_next = (wide + dot(seen, oout_ref[...])).astype(BF16)
        merged = (fine[...].astype(F32) + dot(spread[...], coarse_next)).astype(BF16).astype(F32)
        opad[1 : lats + 1, RIM : RIM + win] = merged.reshape(lats, win, LANES)
        sendb[m] = nine_taps(opad, 2, lats, 2 * RIM, piece).reshape(sendb.shape[1:])
        for step in range(1, n_lat):
            back_copy(m, step).start()
        recvb[m, lat] = sendb[m, lat]
        return carry

    lax.fori_loop(0, members, ocean, 0)

    def finish(m, carry):
        for step in range(1, n_lat):
            back_copy(m, step).wait_recv()
        for origin in range(n_lat):
            landed = recvb[m, origin].astype(F32)
            for r in range(rows):
                at = r * length + origin * piece
                act[at : at + piece] = landed[r * piece : (r + 1) * piece]
        lifted = gelu(dot(act[...].astype(BF16), point_ref[2]))
        sea = seab[...]
        updated = (sea * (start[m].astype(F32) + lifted)).astype(BF16)
        seaside_ref[m] = updated.reshape(rows, length, LANES)
        back = dot(updated, return_ref[...])
        for c in range(chunks):
            cols = slice(c * LANES, (c + 1) * LANES)
            final = cur[blocks, m, :, :, cols].astype(F32).reshape(cells, LANES)
            air = (final + sea * back[:, cols]).astype(BF16)
            air_ref[m, :, :, cols] = air.reshape(rows, length, LANES)
        for step in range(1, n_lat):
            piece_copy(m, step).wait_send()
            back_copy(m, step).wait_send()
        for side in range(2):
            edge_copy(m, side).wait_send()
        for b in range(blocks):
            each_halo(b, m, lambda copy: copy.wait_send(), False)
        return carry

    lax.fori_loop(0, members, finish, 0)


def per_device(sizes, *args):
    atm, prev = args[0], args[1]
    members, rows, length, width = atm.shape
    channels = prev.shape[-1]
    blocks = args[4].shape[0]
    hidden = args[12].shape[2]
    n_lat = sizes[0]
    piece = length // n_lat
    win = -(-(piece + 2 * RIM) // 16) * 16
    lats = rows * n_lat
    args = list(args)
    args[17] = args[17].reshape(1, channels)
    args[4] = args[4].transpose(1, 2, 0, 3)
    vmem = pl.BlockSpec(memory_space=pltpu.VMEM)
    specs = [pl.BlockSpec(memory_space=pltpu.HBM)] * len(args)
    kept = [
        (pltpu.SMEM if index in (7, 19) else pltpu.VMEM)(arg.shape, arg.dtype)
        for index, arg in enumerate(args)
    ]
    dma = pltpu.SemaphoreType.DMA
    return pl.pallas_call(
        functools.partial(kernel, sizes),
        out_shape=(
            jax.ShapeDtypeStruct(atm.shape, BF16),
            jax.ShapeDtypeStruct(prev.shape, BF16),
        ),
        in_specs=specs,
        out_specs=(vmem, vmem),
        scratch_shapes=kept[1:]
        + [
            pltpu.VMEM((blocks + 1,) + atm.shape, BF16),
            pltpu.VMEM((blocks, members, 2, length, width), BF16),
            pltpu.VMEM((blocks, members, 2, rows, EDGE, width), BF16),
            pltpu.VMEM((blocks, members, 4, EDGE, width), BF16),
            pltpu.VMEM((rows + 2, length + 2 * RIM, width), F32),
            pltpu.VMEM((rows * length, width), F32),
            pltpu.VMEM((rows * length, width), BF16),
            pltpu.VMEM((rows, length, length), F32),
            pltpu.VMEM((rows * length, channels), F32),
            pltpu.VMEM((members, rows * length, channels), BF16),
            pltpu.VMEM((rows, length + win, channels), F32),
            pltpu.VMEM((members, n_lat, rows, win, channels), BF16),
            pltpu.VMEM((members, n_lat, rows, win, channels), BF16),
            pltpu.VMEM((members, 2, rows, EDGE, channels), BF16),
            pltpu.VMEM((members, n_lat, rows, EDGE, channels), BF16),
            pltpu.VMEM((lats + 2, win + 2 * RIM, channels), F32),
            pltpu.VMEM((lats // 2 + 2, win // 2 + 2 * RIM, channels), F32),
            pltpu.VMEM((lats * win, channels), BF16),
            pltpu.VMEM((members, n_lat, rows * piece, channels), BF16),
            pltpu.VMEM((members, n_lat, rows * piece, channels), BF16),
            pltpu.VMEM((rows * length, channels), F32),
            pltpu.VMEM((lats * win // 4, lats * win), BF16),
            pltpu.VMEM((lats * win, lats * win // 4), BF16),
            pltpu.VMEM((lats * win // 4, lats * win // 4), F32),
            pltpu.VMEM((rows * length, hidden), BF16),
            dma((len(args),)),
            dma((blocks, members, len(SIDES))),
            dma((blocks, members, len(SIDES))),
            dma((members, n_lat)),
            dma((members, n_lat)),
            dma((members, 2)),
            dma((members, n_lat)),
            dma((members, n_lat)),
            dma((members, n_lat)),
        ],
        compiler_params=pltpu.CompilerParams(
            collective_id=0, has_side_effects=True, vmem_limit_bytes=64 * 2**20
        ),
        cost_estimate=pl.CostEstimate(
            flops=4 * 10**9, bytes_accessed=10**7, transcendentals=2 * 10**6
        ),
    )(*args)


def solution(mesh):
    sizes = tuple(mesh.shape[axis] for axis in ("lat", "lon", "comp"))
    field = P(None, "lat", ("lon", "comp"), None)
    plane = P("lat", ("lon", "comp"))
    return jax.shard_map(
        functools.partial(per_device, sizes),
        mesh=mesh,
        in_specs=(field, field, plane, plane) + (P(),) * 18,
        out_specs=(field, field),
        check_vma=False,
    )
```
